768 devices in a mesh: comp: 32 (over x, y), tile: 24 (over z, core).
Axes of the slice: x: 4, y: 8, z: 12, core: 2. Of those that a mesh axis runs over, the one named last changes fastest.
Arguments:
- atm_state: float32 [128, 512, 3072], P(None, 'comp', 'tile'), may hold values from -6 to 6
- ocean_state: float32 [48, 512, 3072], P(None, 'comp', 'tile'), may hold values from -6 to 6
- atm_rate: float32 [128], replicated, may hold values from 0.02 to 0.24
- ocean_rate: float32 [48], replicated, may hold values from 0.02 to 0.24
- ocean_mask: int32 [512, 24], P('comp', 'tile'), may hold values 0 or 1
- remap_weight: bfloat16 [32, 1152, 128, 128], P('comp', 'tile'), may hold values from -0.5 to 0.5
- pair_src: int32 [32, 1152], P('comp', 'tile'), may hold values from 0 to 383, as said below
- pair_tgt: int32 [32, 1152], P('comp', 'tile'), may hold values from 0 to 383, as said below
- pair_count: int32 [32, 24], P('comp', 'tile'), may hold values from 24 to 48, as said below
Outputs:
- atm_next: float32 [128, 512, 3072], P(None, 'comp', 'tile')
- ocean_next: float32 [48, 512, 3072], P(None, 'comp', 'tile')
The draws below stay inside these ranges and needn't reach their ends.
Inputs may be any that keep to these rules, and one draw needn't show every extreme that they name: `pair_src`: entry d * 48 + j of row b names atmosphere tile e * 16 + y of band b. Among the first pair_count[b, d] entries of device d at most 3 have the same e, and every device has 3 live entries with one same e. `pair_tgt`: entry d * 48 + j of row b names ocean tile e * 16 + y of band b. Among the first pair_count[b, d] entries of device d at most 3 have the same e, and every device has 3 live entries with one same e. `pair_count`: each row b has some device with 48 live slots.
All inputs are finite; a program needn't handle non-finite values. No bound on the sum of `ocean_mask` on one device may be relied on, other than what follows from the above.
Results may differ from the reference program's by a relative error of at most 0.002.
Values may be sent and summed in bfloat16 or wider, within the bound.
A program may use at most 32 MiB of HBM per device.

```python
import math
import jax
import jax.numpy as jnp
from jax import lax

SURF = 8
TILE = 128
AY = 16
OY = 16
PAIRS = 48
CAP = 3
CH_A = 128
CH_O = 48
NY = 512
NOY = 512
NX = 3072
N_COMP = 32
N_TILE = 24


def routed_tiles(base_key, salt_value, row_count):
    salted = jax.random.fold_in(base_key, salt_value)
    first_key, second_key, third_key = jax.random.split(salted, 3)
    slot_total = N_TILE * CAP
    slot_index = jnp.arange(slot_total, dtype=jnp.int32)
    raw_score = jax.random.randint(first_key, (N_COMP, N_TILE, slot_total), 0, 1 << 16)
    full_peer = jax.random.randint(second_key, (N_COMP, N_TILE, 1), 0, N_TILE)
    ordered = jnp.where(slot_index // CAP == full_peer, slot_index - slot_total, raw_score * slot_total + slot_index)
    chosen = jnp.argsort(ordered, axis=-1, stable=True)[..., :PAIRS].astype(jnp.int32)
    offset = jax.random.randint(third_key, (N_COMP, N_TILE, PAIRS), 0, row_count)
    return (chosen // CAP * row_count + offset).reshape(N_COMP, N_TILE * PAIRS).astype(jnp.int32)


def draw_pair_src(key, part):
    return routed_tiles(key, 11, AY)


def draw_pair_tgt(key, part):
    return routed_tiles(key, 23, OY)


def draw_pair_count(key, part):
    salted = jax.random.fold_in(key, 37)
    first_key, second_key = jax.random.split(salted, 2)
    lowest = max(CAP, PAIRS // 2)
    spread_total = PAIRS - lowest
    raw_value = jax.random.randint(first_key, (N_COMP, N_TILE), 0, spread_total + 1)
    counted = lowest + raw_value * raw_value // max(spread_total, 1)
    busiest = jax.random.randint(second_key, (N_COMP, 1), 0, N_TILE)
    device_index = jnp.arange(N_TILE, dtype=jnp.int32)[None, :]
    return jnp.where(device_index == busiest, PAIRS, jnp.minimum(counted, PAIRS)).astype(jnp.int32)


def plant(array, key, low, top_value):
    longest = array.shape.index(max(array.shape))
    spots = []
    for shift in (0, 1):
        where = [jax.random.randint(jax.random.fold_in(key, axis), (), 0, length) for axis, length in enumerate(array.shape)]
        where[longest] = (where[longest] + shift) % array.shape[longest]
        spots.append(tuple(where))
    return array.at[spots[0]].set(low).at[spots[1]].set(top_value)


def level_of(own_key, shape, shards, low, largest):
    loudness, own = 1.0, jax.random.fold_in(own_key, 6)
    for axis_at, blocks in shards:
        draws = jnp.exp(jax.random.uniform(jax.random.fold_in(own, axis_at), (blocks,), jnp.float32, low / len(shards), largest / len(shards)))
        loudness = loudness * jnp.repeat(draws, shape[axis_at] // blocks).reshape([-1 if axis == axis_at else 1 for axis in range(len(shape))])
    return loudness


def centred(stream_key, extent, deviation, most, cuts=(), kind=jnp.bfloat16):
    entries = deviation * jax.random.normal(stream_key, extent, jnp.float32)
    if cuts:
        entries = entries * level_of(stream_key, extent, cuts, -0.22, 0.18)
    return jnp.clip(entries, -most, most).astype(kind)


def setup_inputs(seed: int = 0) -> dict:
    key_list = jax.random.split(jax.random.key(seed), 10)
    return {
        "atm_state": centred(key_list[0], (CH_A, NY, NX), 1.0, 6.0, ((1, 32), (2, 24)), jnp.float32),
        "ocean_state": centred(key_list[1], (CH_O, NOY, NX), 1.0, 6.0, ((1, 32), (2, 24)), jnp.float32),
        "atm_rate": jnp.clip(jnp.exp(jax.random.uniform(key_list[2], (CH_A,), jnp.float32, math.log(0.02), math.log(0.24))), 0.02, 0.24),
        "ocean_rate": jnp.clip(jnp.exp(jax.random.uniform(key_list[3], (CH_O,), jnp.float32, math.log(0.02), math.log(0.24))), 0.02, 0.24),
        "ocean_mask": plant((jax.random.randint(key_list[4], (NOY, N_TILE), 0, 4) < 3).astype(jnp.int32), jax.random.fold_in(key_list[4], 1), 0, 1),
        "remap_weight": centred(key_list[5], (N_COMP, N_TILE * PAIRS, TILE, TILE), TILE ** -0.5, 0.5, ((0, 32), (1, 24))),
        "pair_src": draw_pair_src(jax.random.fold_in(key_list[9], 71), 0),
        "pair_tgt": draw_pair_tgt(jax.random.fold_in(key_list[9], 71), 0),
        "pair_count": draw_pair_count(jax.random.fold_in(key_list[9], 71), 0),
    }


def relax(values, spread):
    padded = jnp.pad(values, ((0, 0), (1, 1), (0, 0)))
    beside_all = padded[:, 2:] + padded[:, :-2] + jnp.roll(values, 1, 2) + jnp.roll(values, -1, 2)
    return values + spread[:, None, None] * (beside_all - 4.0 * values)


def to_tiles(values, row_count):
    shaped = values.reshape(SURF, N_COMP, row_count, N_TILE, TILE)
    return shaped.transpose(1, 3, 2, 0, 4).reshape(N_COMP, N_TILE * row_count, SURF, TILE)


def from_tiles(values, row_count):
    shaped = values.reshape(N_COMP, N_TILE, row_count, SURF, TILE)
    return shaped.transpose(3, 0, 2, 1, 4).reshape(SURF, N_COMP * row_count, N_TILE * TILE)


def reference(atm_state, ocean_state, atm_rate, ocean_rate, ocean_mask, remap_weight, pair_src, pair_tgt, pair_count):
    wet = jnp.repeat(ocean_mask.astype(jnp.float32), TILE, axis=1)
    atm_source = atm_state[:SURF].astype(jnp.bfloat16)
    ocean_source = (ocean_state[:SURF] * wet[None]).astype(jnp.bfloat16)
    atm_tiles = to_tiles(atm_source, AY)
    ocean_tiles = to_tiles(ocean_source, OY)

    def couple(inputs):
        atm_group, ocean_group, weights, anchor, target, live_count = inputs
        active = (jnp.arange(PAIRS)[None, :] < live_count[:, None]).reshape(-1).astype(jnp.float32)
        blocks = weights.astype(jnp.float32)
        forward = jnp.einsum("pft,pts->pfs", atm_group[anchor].astype(jnp.float32), blocks,
                             precision=lax.Precision.HIGHEST) * active[:, None, None]
        reverse = jnp.einsum("pfs,pts->pft", ocean_group[target].astype(jnp.float32), blocks,
                             precision=lax.Precision.HIGHEST) * active[:, None, None]
        ocean_force = jnp.zeros((N_TILE * OY, SURF, TILE), jnp.float32).at[target].add(forward)
        atm_force = jnp.zeros((N_TILE * AY, SURF, TILE), jnp.float32).at[anchor].add(reverse)
        return atm_force, ocean_force

    atm_force, ocean_force = lax.map(couple, (atm_tiles, ocean_tiles, remap_weight, pair_src, pair_tgt, pair_count))
    atm_forcing = from_tiles(atm_force, AY)
    ocean_forcing = from_tiles(ocean_force, OY)
    atm_stepped = relax(relax(atm_state, atm_rate), atm_rate)
    ocean_stepped = relax(relax(ocean_state, ocean_rate), ocean_rate)
    atm_next = atm_stepped.at[:SURF].add(atm_forcing)
    ocean_next = ocean_stepped.at[:SURF].add(ocean_forcing * wet[None])
    return atm_next, ocean_next
```

```python
import functools

import jax
import jax.numpy as jnp
from jax import lax
from jax.experimental import pallas as pl
from jax.experimental.pallas import tpu as pltpu
from jax.sharding import PartitionSpec as P

SURF = 8
LANES = 128
ROWS = 16
CAP = 3
EMPTY = 100.0
F32 = jnp.float32
BF16 = jnp.bfloat16
MESH = pl.DeviceIdType.MESH


def lanes_of(shape):
    return lax.broadcasted_iota(jnp.int32, shape, 1)


def rows_of(shape):
    return lax.broadcasted_iota(jnp.int32, shape, 0)


def as_column(row, size):
    shape = (size, size)
    spread = jnp.broadcast_to(row, shape)
    zero = jnp.zeros(shape, row.dtype)
    return jnp.sum(jnp.where(rows_of(shape) == lanes_of(shape), spread, zero), axis=1, keepdims=True)


def as_row(column, size):
    shape = (size, size)
    spread = jnp.broadcast_to(column, shape)
    zero = jnp.zeros(shape, column.dtype)
    return jnp.sum(jnp.where(rows_of(shape) == lanes_of(shape), spread, zero), axis=0, keepdims=True)


def kernel(
    sizes,
    atm_hbm,
    ocean_hbm,
    atm_rate_hbm,
    ocean_rate_hbm,
    mask_hbm,
    weight_hbm,
    pair_src_hbm,
    pair_tgt_hbm,
    pair_count,
    atm_out,
    ocean_out,
    state,
    middle,
    result,
    weight,
    atm_rate,
    ocean_rate,
    mask,
    pair_src,
    pair_tgt,
    band,
    msg_out,
    msg_in,
    meta_out,
    meta_in,
    onehot,
    rate,
    rows_out,
    rows_in,
    cols_out,
    cols_in,
    table_v,
    table_s,
    load_sem,
    ring_send,
    ring_recv,
    sib_recv,
    halo_send,
    halo_recv,
    meta_send,
    meta_recv,
    msg_send,
    msg_recv,
    table_sem,
    out_sem,
):
    n_comp, n_tile, ch_a, ch_o, pairs = sizes
    n_z = n_tile // 2
    hops = n_z // 2
    groups = (ch_a + ch_o) // 8
    a_rows = ch_a * ROWS
    all_rows = (ch_a + ch_o) * ROWS
    s_rows = SURF * ROWS
    slots = n_tile * 8
    comp = lax.axis_index("comp")
    me = lax.axis_index("tile")
    z = me // 2
    core = me % 2
    sibling = z * 2 + 1 - core

    def load(i, src, dst):
        copy = pltpu.make_async_copy(src, dst, load_sem.at[i])
        copy.start()
        return copy

    surf_loads = (
        load(5, mask_hbm, mask),
        load(0, atm_hbm.at[pl.ds(0, s_rows)], state.at[pl.ds(0, s_rows)]),
        load(1, ocean_hbm.at[pl.ds(0, s_rows)], state.at[pl.ds(a_rows, s_rows)]),
    )
    rest_loads = [
        load(2, atm_hbm.at[pl.ds(s_rows, a_rows - s_rows)], state.at[pl.ds(s_rows, a_rows - s_rows)])
    ]
    if ch_o > SURF:
        rest_loads.append(
            load(
                3,
                ocean_hbm.at[pl.ds(s_rows, ch_o * ROWS - s_rows)],
                state.at[pl.ds(a_rows + s_rows, ch_o * ROWS - s_rows)],
            )
        )
    small_loads = [
        load(6, atm_rate_hbm, atm_rate),
        load(7, ocean_rate_hbm, ocean_rate),
        load(8, pair_src_hbm, pair_src),
        load(9, pair_tgt_hbm, pair_tgt),
    ]
    weight_load = load(4, weight_hbm, weight)

    barrier = pltpu.get_barrier_semaphore()
    north = lax.rem(comp + n_comp - 1, n_comp)
    south = lax.rem(comp + 1, n_comp)

    def greet(i, carry):
        pl.semaphore_signal(
            barrier, inc=1, device_id=(comp, lax.rem(me + i, n_tile)), device_id_type=MESH
        )
        return carry

    lax.fori_loop(1, n_tile, greet, 0)
    pl.semaphore_signal(barrier, inc=1, device_id=(north, me), device_id_type=MESH)
    pl.semaphore_signal(barrier, inc=1, device_id=(south, me), device_id_type=MESH)

    for copy in surf_loads:
        copy.wait()
    wet = jnp.broadcast_to(as_column(mask[...].astype(F32), ROWS), (ROWS, LANES))
    own = (core * n_z + z) * ROWS
    for y in range(ROWS):
        atm = state[pl.ds(y, 8, stride=ROWS), :]
        ocean = state[pl.ds(a_rows + y, 8, stride=ROWS), :] * wet[y : y + 1, :]
        band[own + y] = jnp.concatenate([atm, ocean], axis=0).astype(BF16)

    pl.semaphore_wait(barrier, n_tile + 1)

    half = ROWS // 2

    def block(owner_z, c):
        return band.at[pl.ds((core * n_z + owner_z) * ROWS + c * half, half)]

    def used(way, hop, c):
        return hop < hops - 1 or (hop == hops - 1 and c == way)

    def ring_copy(owner_z, way, hop, c):
        step = 1 if way == 0 else n_z - 1
        return pltpu.make_async_remote_copy(
            src_ref=block(owner_z, c),
            dst_ref=block(owner_z, c),
            send_sem=ring_send,
            recv_sem=ring_recv.at[way, hop, c],
            device_id=(comp, lax.rem(z + step, n_z) * 2 + core),
            device_id_type=MESH,
        )

    def sib_copy(owner_z, c):
        return pltpu.make_async_remote_copy(
            src_ref=block(owner_z, c),
            dst_ref=block(owner_z, c),
            send_sem=ring_send,
            recv_sem=sib_recv,
            device_id=(comp, sibling),
            device_id_type=MESH,
        )

    chunks = 0
    for c in range(2):
        for way in range(2):
            if used(way, 0, c):
                ring_copy(z, way, 0, c).start()
                chunks += 1
    for c in range(2):
        sib_copy(z, c).start()
        chunks += 1

    def service(hop):
        count = 0
        for c in range(2):
            for way in range(2):
                if not used(way, hop, c):
                    continue
                back = n_z - (hop + 1) if way == 0 else hop + 1
                owner_z = lax.rem(z + back, n_z)
                ring_copy(owner_z, way, hop, c).wait_recv()
                if used(way, hop + 1, c):
                    ring_copy(owner_z, way, hop + 1, c).start()
                    count += 1
                sib_copy(owner_z, c).start()
                count += 1
        return count

    lane8 = lanes_of((8, LANES))

    def pack(g, rows, turn):
        west = jnp.zeros((8, LANES), F32)
        east = jnp.zeros((8, LANES), F32)
        for y in range(ROWS):
            here = lane8 == y
            west = jnp.where(here, rows[y] if y == 0 else pltpu.roll(rows[y], y, 1), west)
            east = jnp.where(here, pltpu.roll(rows[y], y + 1, 1), east)
        shift = lax.rem(g, 8) * ROWS
        at = pl.ds(pl.multiple_of(g // 8 * 8, 8), 8)
        cols_out[turn, 0, at, :] = cols_out[turn, 0, at, :] + pltpu.roll(west, shift, 1)
        cols_out[turn, 1, at, :] = cols_out[turn, 1, at, :] + pltpu.roll(east, shift, 1)
        own8 = pl.ds(pl.multiple_of(g * 8, 8), 8)
        rows_out[turn, 0, own8, :] = rows[0]
        rows_out[turn, 1, own8, :] = rows[ROWS - 1]

    def group_rows(ref, g):
        return [ref[pl.ds(g * LANES + y, 8, stride=ROWS), :] for y in range(ROWS)]

    def halo_copies(turn):
        west_of, east_of = lax.rem(me + n_tile - 1, n_tile), lax.rem(me + 1, n_tile)
        plan = (
            (rows_out.at[turn, 0], rows_in.at[turn, 1], (north, me)),
            (rows_out.at[turn, 1], rows_in.at[turn, 0], (south, me)),
            (cols_out.at[turn, 0], cols_in.at[turn, 1], (comp, west_of)),
            (cols_out.at[turn, 1], cols_in.at[turn, 0], (comp, east_of)),
        )
        return [
            pltpu.make_async_remote_copy(
                src_ref=src,
                dst_ref=dst,
                send_sem=halo_send.at[turn, i],
                recv_sem=halo_recv.at[turn, i],
                device_id=to,
                device_id_type=MESH,
            )
            for i, (src, dst, to) in enumerate(plan)
        ]

    keep_north = (comp > 0).astype(F32)
    keep_south = (comp < n_comp - 1).astype(F32)

    def relax_group(g, source, target, turn):
        rows = group_rows(source, g)
        own8 = pl.ds(pl.multiple_of(g * 8, 8), 8)
        above = rows_in[turn, 0, own8, :] * keep_north
        below = rows_in[turn, 1, own8, :] * keep_south
        at = pl.ds(pl.multiple_of(g // 8 * 8, 8), 8)
        shift = lax.rem(LANES - lax.rem(g, 8) * ROWS, LANES)
        west = pltpu.roll(cols_in[turn, 0, at, :], shift, 1)
        east = pltpu.roll(cols_in[turn, 1, at, :], shift, 1)
        spread = rate[own8, :]
        new = []
        for y in range(ROWS):
            row = rows[y]
            left = pltpu.roll(
                jnp.where(lane8 == LANES - 1, pltpu.roll(west, LANES - 1 - y, 1), row), 1, 1
            )
            beyond = east if y == 0 else pltpu.roll(east, LANES - y, 1)
            right = pltpu.roll(jnp.where(lane8 == 0, beyond, row), LANES - 1, 1)
            up = above if y == 0 else rows[y - 1]
            down = below if y == ROWS - 1 else rows[y + 1]
            value = row + spread * (up + down + left + right - 4.0 * row)
            target[pl.ds(g * LANES + y, 8, stride=ROWS), :] = value
            new.append(value)
        return new

    cols_out[...] = jnp.zeros_like(cols_out)
    for copy in rest_loads:
        copy.wait()

    def first_pack(g, carry):
        pack(g, group_rows(state, g), 0)
        return carry

    lax.fori_loop(0, groups, first_pack, 0)
    halo_first = halo_copies(0)
    for copy in halo_first:
        copy.start()

    for copy in small_loads:
        copy.wait()
    rate[pl.ds(0, ch_a), :] = jnp.broadcast_to(as_column(atm_rate[...], ch_a), (ch_a, LANES))
    rate[pl.ds(ch_a, ch_o), :] = jnp.broadcast_to(as_column(ocean_rate[...], ch_o), (ch_o, LANES))

    pair_shape = (pairs, pairs)
    later = lanes_of(pair_shape) < rows_of(pair_shape)
    live_row = (lanes_of((1, pairs)) < pair_count[0, 0]).astype(jnp.int32)
    live_column = (rows_of((pairs, 1)) < pair_count[0, 0]).astype(jnp.int32)
    live_all = jnp.broadcast_to(live_row, pair_shape)
    pair_column = rows_of((pairs, 1))
    slot_lane = lanes_of((pairs, slots))
    slot_row = rows_of((slots, pairs))
    place, lines, y_of = [], [], []
    for codes in (pair_tgt, pair_src):
        code = codes[...]
        peer = code >> 4
        y_row = (code & 15).astype(F32)
        tile = ((peer & 1) * n_z + (peer >> 1)) * ROWS + (code & 15)
        peer_column = as_column(peer, pairs)
        before = jnp.logical_and(later, jnp.broadcast_to(peer, pair_shape) == peer_column)
        rank_column = jnp.sum(
            jnp.where(before, live_all, jnp.zeros_like(live_all)), axis=1, keepdims=True
        )
        rank_row = as_row(rank_column, pairs)
        slot_column = jnp.where(live_column > 0, peer_column * 8 + rank_column, -1)
        slot_of_row = jnp.where(live_row > 0, peer * 8 + rank_row, -1)
        place.append(as_column(tile, pairs))
        lines.append(slot_column == slot_lane)
        hot_rows = jnp.where(slot_row == slot_of_row, y_row - EMPTY, 0.0)
        y_of.append(jnp.sum(hot_rows, axis=1, keepdims=True) + EMPTY)
    table_v[...] = jnp.zeros_like(table_v)
    for i, (hot, values) in enumerate(
        ((lines[0], pair_column), (lines[0], place[1]), (lines[1], pair_column), (lines[1], place[0]))
    ):
        found = jnp.where(hot, jnp.broadcast_to(values, (pairs, slots)), jnp.zeros_like(slot_lane))
        table_v[i : i + 1, :] = jnp.sum(found, axis=0, keepdims=True)
    table_copy = pltpu.make_async_copy(table_v, table_s, table_sem)
    table_copy.start()
    meta_lane = lanes_of((slots, LANES))
    inside = (meta_lane >> 4) == lax.rem(me, 8)
    meta_out[...] = jnp.where(
        inside,
        jnp.where((meta_lane & 15) < 8, y_of[0], y_of[1]),
        0.0,
    )

    def meta_slot(e):
        return pl.ds(pl.multiple_of(e * 8, 8), 8)

    def send_meta(i, carry):
        e = lax.rem(me + i, n_tile)
        pltpu.make_async_remote_copy(
            src_ref=meta_out.at[meta_slot(e)],
            dst_ref=meta_in.at[meta_slot(me)],
            send_sem=meta_send,
            recv_sem=meta_recv,
            device_id=(comp, e),
            device_id_type=MESH,
        ).start()
        return carry

    lax.fori_loop(1, n_tile, send_meta, 0)
    pltpu.make_async_copy(
        meta_out.at[meta_slot(me)], meta_in.at[meta_slot(me)], meta_recv
    ).start()

    def first_step(g, carry):
        pack(g, relax_group(g, state, middle, 0), 1)
        return carry

    def second_step(g, carry):
        relax_group(g, middle, result, 1)
        return carry

    def build_onehot():
        pltpu.make_async_copy(meta_in, meta_in, meta_recv).wait()
        shape = (2 * s_rows, LANES)
        y_at = (rows_of(shape) & 15).astype(F32)
        field = rows_of(shape) >> 4
        same = field == (lanes_of(shape) & 15)
        per = min(8, n_tile)
        for part in range(n_tile // per):
            total = meta_in[pl.ds(part * per * 8, 8), :]
            for d in range(1, per):
                total = total + meta_in[pl.ds((part * per + d) * 8, 8), :]
            for r in range(CAP):
                hit = jnp.logical_and(same, total[r : r + 1, :] == y_at)
                start = r * n_tile * ROWS + part * LANES
                onehot[:, start : start + LANES] = jnp.where(hit, 1.0, 0.0).astype(BF16)

    done = []

    def halo_wait(copies):
        for copy in copies:
            copy.wait()

    cut = min(groups // 2, ch_a // 8)

    def work_a():
        halo_wait(halo_first)
        lax.fori_loop(0, cut, first_step, 0)

    def work_b():
        lax.fori_loop(cut, groups, first_step, 0)
        copies = halo_copies(1)
        for copy in copies:
            copy.start()
        done.append(copies)

    def work_c():
        halo_wait(done[0])
        lax.fori_loop(0, cut, second_step, 0)

    def work_d():
        lax.fori_loop(cut, groups, second_step, 0)

    stages = [work_a, work_b, build_onehot, work_c, work_d]
    for hop in range(hops):
        chunks += service(hop)
        if stages:
            stages.pop(0)()
    for stage in stages:
        stage()

    def write(i, src_row, dst, dst_row, size):
        copy = pltpu.make_async_copy(
            result.at[pl.ds(src_row, size)], dst.at[pl.ds(dst_row, size)], out_sem.at[i]
        )
        copy.start()
        return copy

    writes = [write(0, s_rows, atm_out, s_rows, a_rows - s_rows)]
    if ch_o > SURF:
        writes.append(write(1, a_rows + s_rows, ocean_out, s_rows, ch_o * ROWS - s_rows))

    weight_load.wait()
    table_copy.wait()
    theirs = band.at[pl.ds((1 - core) * n_z * ROWS, n_z * ROWS)]
    pltpu.make_async_copy(theirs, theirs, sib_recv).wait()

    top = rows_of((ROWS, LANES)) < 8

    def msg_slot(e):
        return pl.ds(pl.multiple_of(e * ROWS, ROWS), ROWS)

    def fill(e):
        for r in range(CAP):
            s = e * 8 + r
            ahead = jnp.dot(
                band[table_s[1, s]], weight[table_s[0, s]], preferred_element_type=F32
            )
            back = lax.dot_general(
                band[table_s[3, s]],
                weight[table_s[2, s]],
                (((1,), (1,)), ((), ())),
                preferred_element_type=F32,
            )
            msg_out[msg_slot(e), r * LANES : (r + 1) * LANES] = jnp.where(top, ahead, back).astype(
                BF16
            )

    def send(e):
        pltpu.make_async_remote_copy(
            src_ref=msg_out.at[msg_slot(e)],
            dst_ref=msg_in.at[msg_slot(me)],
            send_sem=msg_send,
            recv_sem=msg_recv,
            device_id=(comp, e),
            device_id_type=MESH,
        ).start()

    def far_to_near(i, carry):
        away = hops - (i + 1) // 2
        away = jnp.where(lax.rem(i, 2) == 1, away, n_z - away)
        other = lax.rem(z + away, n_z) * 2
        for k in range(2):
            fill(other + k)
            send(other + k)
        return carry

    lax.fori_loop(0, n_z - 1, far_to_near, 0)
    fill(sibling)
    send(sibling)
    fill(me)
    pltpu.make_async_copy(msg_out.at[msg_slot(me)], msg_in.at[msg_slot(me)], msg_recv).start()

    pltpu.make_async_copy(msg_in, msg_in, msg_recv).wait()
    force = jnp.zeros((2 * s_rows, LANES), F32)
    depth = n_tile * ROWS
    for r in range(CAP):
        force = force + jnp.dot(
            onehot[:, r * depth : (r + 1) * depth],
            msg_in[:, r * LANES : (r + 1) * LANES],
            preferred_element_type=F32,
        )
    wet_rows = jnp.concatenate([wet] * SURF, axis=0)
    result[pl.ds(0, s_rows), :] = result[pl.ds(0, s_rows), :] + force[s_rows:]
    writes.append(write(2, 0, atm_out, 0, s_rows))
    result[pl.ds(a_rows, s_rows), :] = result[pl.ds(a_rows, s_rows), :] + force[:s_rows] * wet_rows
    writes.append(write(3, a_rows, ocean_out, 0, s_rows))

    sent = band.at[pl.ds(0, chunks * half)]
    pltpu.make_async_copy(sent, sent, ring_send).wait()
    metas = meta_out.at[pl.ds(0, (n_tile - 1) * 8)]
    pltpu.make_async_copy(metas, metas, meta_send).wait()
    msgs = msg_out.at[pl.ds(0, (n_tile - 1) * ROWS)]
    pltpu.make_async_copy(msgs, msgs, msg_send).wait()
    for copy in writes:
        copy.wait()


def shards(
    n_comp,
    n_tile,
    atm_state,
    ocean_state,
    atm_rate,
    ocean_rate,
    ocean_mask,
    remap_weight,
    pair_src,
    pair_tgt,
    pair_count,
):
    ch_a, ch_o = atm_state.shape[0], ocean_state.shape[0]
    pairs = pair_src.shape[1]
    total = ch_a + ch_o
    a_rows, o_rows = ch_a * ROWS, ch_o * ROWS
    hops = n_tile // 4
    packed = (total // 8 + 7) // 8 * 8
    hbm = pl.BlockSpec(memory_space=pltpu.HBM)
    dma = pltpu.SemaphoreType.DMA
    atm_next, ocean_next = pl.pallas_call(
        functools.partial(kernel, (n_comp, n_tile, ch_a, ch_o, pairs)),
        out_shape=(
            jax.ShapeDtypeStruct((a_rows, LANES), F32),
            jax.ShapeDtypeStruct((o_rows, LANES), F32),
        ),
        in_specs=[hbm] * 8 + [pl.BlockSpec(memory_space=pltpu.SMEM)],
        out_specs=(hbm, hbm),
        scratch_shapes=[
            pltpu.VMEM((total * ROWS + ROWS, LANES), F32),
            pltpu.VMEM((total * ROWS + ROWS, LANES), F32),
            pltpu.VMEM((total * ROWS + ROWS, LANES), F32),
            pltpu.VMEM((pairs, LANES, LANES), BF16),
            pltpu.VMEM((1, ch_a), F32),
            pltpu.VMEM((1, ch_o), F32),
            pltpu.VMEM((1, ROWS), jnp.int32),
            pltpu.VMEM((1, pairs), jnp.int32),
            pltpu.VMEM((1, pairs), jnp.int32),
            pltpu.VMEM((n_tile * ROWS, 2 * SURF, LANES), BF16),
            pltpu.VMEM((n_tile * ROWS, CAP * LANES), BF16),
            pltpu.VMEM((n_tile * ROWS, CAP * LANES), BF16),
            pltpu.VMEM((n_tile * 8, LANES), F32),
            pltpu.VMEM((n_tile * 8, LANES), F32),
            pltpu.VMEM((2 * SURF * ROWS, CAP * n_tile * ROWS), BF16),
            pltpu.VMEM((total, LANES), F32),
            pltpu.VMEM((2, 2, total, LANES), F32),
            pltpu.VMEM((2, 2, total, LANES), F32),
            pltpu.VMEM((2, 2, packed, LANES), F32),
            pltpu.VMEM((2, 2, packed, LANES), F32),
            pltpu.VMEM((8, n_tile * 8), jnp.int32),
            pltpu.SMEM((8, n_tile * 8), jnp.int32),
            dma((10,)),
            dma,
            dma((2, hops, 2)),
            dma,
            dma((2, 4)),
            dma((2, 4)),
            dma,
            dma,
            dma,
            dma,
            dma,
            dma((4,)),
        ],
        compiler_params=pltpu.CompilerParams(
            collective_id=0, has_side_effects=True, vmem_limit_bytes=60 * 1024 * 1024
        ),
        name="coupled_interval",
    )(
        atm_state.reshape(a_rows, LANES),
        ocean_state.reshape(o_rows, LANES),
        atm_rate.reshape(1, ch_a),
        ocean_rate.reshape(1, ch_o),
        ocean_mask.reshape(1, ROWS),
        remap_weight.reshape(pairs, LANES, LANES),
        pair_src,
        pair_tgt,
        pair_count,
    )
    return atm_next.reshape(ch_a, ROWS, LANES), ocean_next.reshape(ch_o, ROWS, LANES)


def solution(mesh):
    return jax.shard_map(
        functools.partial(shards, mesh.shape["comp"], mesh.shape["tile"]),
        mesh=mesh,
        in_specs=(
            P(None, "comp", "tile"),
            P(None, "comp", "tile"),
            P(),
            P(),
            P("comp", "tile"),
            P("comp", "tile", None, None),
            P("comp", "tile"),
            P("comp", "tile"),
            P("comp", "tile"),
        ),
        out_specs=(P(None, "comp", "tile"), P(None, "comp", "tile")),
        check_vma=False,
    )
```

```python
import functools

import jax
import jax.numpy as jnp
from jax import lax
from jax.experimental import pallas as pl
from jax.experimental.pallas import tpu as pltpu
from jax.sharding import PartitionSpec as P

SURF = 8
LANES = 128
ROWS = 16
CAP = 3
EMPTY = 16
F32 = jnp.float32
BF16 = jnp.bfloat16
MESH = pl.DeviceIdType.MESH


def lanes_of(shape):
    return lax.broadcasted_iota(jnp.int32, shape, 1)


def rows_of(shape):
    return lax.broadcasted_iota(jnp.int32, shape, 0)


def as_column(row, size):
    shape = (size, size)
    spread = jnp.broadcast_to(row, shape)
    zero = jnp.zeros(shape, row.dtype)
    return jnp.sum(jnp.where(rows_of(shape) == lanes_of(shape), spread, zero), axis=1, keepdims=True)


def as_row(column, size):
    shape = (size, size)
    spread = jnp.broadcast_to(column, shape)
    zero = jnp.zeros(shape, column.dtype)
    return jnp.sum(jnp.where(rows_of(shape) == lanes_of(shape), spread, zero), axis=0, keepdims=True)


def kernel(
    sizes,
    atm_hbm,
    ocean_hbm,
    atm_rate_hbm,
    ocean_rate_hbm,
    mask_hbm,
    weight_hbm,
    pair_src_hbm,
    pair_tgt_hbm,
    pair_count,
    atm_out,
    ocean_out,
    state,
    middle,
    result,
    weight,
    atm_rate,
    ocean_rate,
    mask,
    pair_src,
    pair_tgt,
    own,
    tile_out,
    tile_in,
    msg_out,
    msg_in,
    meta_out,
    meta_in,
    onehot,
    rate,
    rows_out,
    rows_in,
    cols_out,
    cols_in,
    table_v,
    table_s,
    asked_v,
    asked_s,
    load_sem,
    tile_send,
    tile_recv,
    halo_send,
    halo_recv,
    meta_send,
    meta_recv,
    msg_send,
    msg_recv,
    table_sem,
    asked_sem,
    out_sem,
):
    n_comp, n_tile, ch_a, ch_o, pairs = sizes
    n_z = n_tile // 2
    hops = n_z // 2
    groups = (ch_a + ch_o) // 8
    a_rows = ch_a * ROWS
    all_rows = (ch_a + ch_o) * ROWS
    s_rows = SURF * ROWS
    slots = n_tile * 8
    comp = lax.axis_index("comp")
    me = lax.axis_index("tile")
    z = me // 2
    core = me % 2
    sibling = z * 2 + 1 - core

    def load(i, src, dst):
        copy = pltpu.make_async_copy(src, dst, load_sem.at[i])
        copy.start()
        return copy

    surf_loads = (
        load(5, mask_hbm, mask),
        load(0, atm_hbm.at[pl.ds(0, s_rows)], state.at[pl.ds(0, s_rows)]),
        load(1, ocean_hbm.at[pl.ds(0, s_rows)], state.at[pl.ds(a_rows, s_rows)]),
    )
    rest_loads = [
        load(2, atm_hbm.at[pl.ds(s_rows, a_rows - s_rows)], state.at[pl.ds(s_rows, a_rows - s_rows)])
    ]
    if ch_o > SURF:
        rest_loads.append(
            load(
                3,
                ocean_hbm.at[pl.ds(s_rows, ch_o * ROWS - s_rows)],
                state.at[pl.ds(a_rows + s_rows, ch_o * ROWS - s_rows)],
            )
        )
    small_loads = [
        load(6, atm_rate_hbm, atm_rate),
        load(7, ocean_rate_hbm, ocean_rate),
        load(8, pair_src_hbm, pair_src),
        load(9, pair_tgt_hbm, pair_tgt),
    ]
    weight_load = load(4, weight_hbm, weight)

    barrier = pltpu.get_barrier_semaphore()
    north = lax.rem(comp + n_comp - 1, n_comp)
    south = lax.rem(comp + 1, n_comp)

    def greet(i, carry):
        pl.semaphore_signal(
            barrier, inc=1, device_id=(comp, lax.rem(me + i, n_tile)), device_id_type=MESH
        )
        return carry

    lax.fori_loop(1, n_tile, greet, 0)
    pl.semaphore_signal(barrier, inc=1, device_id=(north, me), device_id_type=MESH)
    pl.semaphore_signal(barrier, inc=1, device_id=(south, me), device_id_type=MESH)

    for copy in small_loads:
        copy.wait()

    pair_shape = (pairs, pairs)
    later = lanes_of(pair_shape) < rows_of(pair_shape)
    live_row = (lanes_of((1, pairs)) < pair_count[0, 0]).astype(jnp.int32)
    live_column = (rows_of((pairs, 1)) < pair_count[0, 0]).astype(jnp.int32)
    live_all = jnp.broadcast_to(live_row, pair_shape)
    pair_column = rows_of((pairs, 1))
    slot_lane = lanes_of((pairs, slots))
    slot_row = rows_of((slots, pairs))
    place, lines, y_of = [], [], []
    for codes in (pair_tgt, pair_src):
        code = codes[...]
        peer = code >> 4
        y_row = code & 15
        peer_column = as_column(peer, pairs)
        before = jnp.logical_and(later, jnp.broadcast_to(peer, pair_shape) == peer_column)
        rank_column = jnp.sum(
            jnp.where(before, live_all, jnp.zeros_like(live_all)), axis=1, keepdims=True
        )
        rank_row = as_row(rank_column, pairs)
        slot_column = jnp.where(live_column > 0, peer_column * 8 + rank_column, -1)
        slot_of_row = jnp.where(live_row > 0, peer * 8 + rank_row, -1)
        place.append(peer_column * CAP + rank_column)
        lines.append(slot_column == slot_lane)
        hot_rows = jnp.where(slot_row == slot_of_row, jnp.broadcast_to(y_row - EMPTY, (slots, pairs)), jnp.zeros_like(slot_row))
        y_of.append(jnp.sum(hot_rows, axis=1, keepdims=True) + EMPTY)
    table_v[...] = jnp.zeros_like(table_v)
    for i, (hot, values) in enumerate(
        ((lines[0], pair_column), (lines[0], place[1]), (lines[1], pair_column), (lines[1], place[0]))
    ):
        found = jnp.where(hot, jnp.broadcast_to(values, (pairs, slots)), jnp.zeros_like(slot_lane))
        table_v[i : i + 1, :] = jnp.sum(found, axis=0, keepdims=True)
    table_copy = pltpu.make_async_copy(table_v, table_s, table_sem)
    table_copy.start()
    meta_lane = lanes_of((slots, LANES))
    inside = (meta_lane >> 4) == lax.rem(me, 8)
    meta_out[...] = jnp.where(
        inside,
        jnp.where(
            (meta_lane & 15) < 8,
            jnp.broadcast_to(y_of[0], (slots, LANES)),
            jnp.broadcast_to(y_of[1], (slots, LANES)),
        ),
        jnp.zeros_like(meta_lane),
    )

    def meta_slot(e):
        return pl.ds(pl.multiple_of(e * 8, 8), 8)

    def send_meta(i, carry):
        e = lax.rem(me + i, n_tile)
        pltpu.make_async_remote_copy(
            src_ref=meta_out.at[meta_slot(e)],
            dst_ref=meta_in.at[meta_slot(me)],
            send_sem=meta_send,
            recv_sem=meta_recv,
            device_id=(comp, e),
            device_id_type=MESH,
        ).start()
        return carry

    pl.semaphore_wait(barrier, n_tile + 1)
    lax.fori_loop(1, n_tile, send_meta, 0)
    pltpu.make_async_copy(
        meta_out.at[meta_slot(me)], meta_in.at[meta_slot(me)], meta_recv
    ).start()

    for copy in surf_loads:
        copy.wait()
    wet = jnp.broadcast_to(as_column(mask[...].astype(F32), ROWS), (ROWS, LANES))
    for y in range(ROWS):
        air = state[pl.ds(y, 8, stride=ROWS), :]
        sea = state[pl.ds(a_rows + y, 8, stride=ROWS), :] * wet[y : y + 1, :]
        own[y] = jnp.concatenate([air, sea], axis=0).astype(BF16)


    lane8 = lanes_of((8, LANES))

    def pack(g, rows, turn):
        west = jnp.zeros((8, LANES), F32)
        east = jnp.zeros((8, LANES), F32)
        for y in range(ROWS):
            here = lane8 == y
            west = jnp.where(here, rows[y] if y == 0 else pltpu.roll(rows[y], y, 1), west)
            east = jnp.where(here, pltpu.roll(rows[y], y + 1, 1), east)
        shift = lax.rem(g, 8) * ROWS
        at = pl.ds(pl.multiple_of(g // 8 * 8, 8), 8)
        cols_out[turn, 0, at, :] = cols_out[turn, 0, at, :] + pltpu.roll(west, shift, 1)
        cols_out[turn, 1, at, :] = cols_out[turn, 1, at, :] + pltpu.roll(east, shift, 1)
        own8 = pl.ds(pl.multiple_of(g * 8, 8), 8)
        rows_out[turn, 0, own8, :] = rows[0]
        rows_out[turn, 1, own8, :] = rows[ROWS - 1]

    def group_rows(ref, g):
        return [ref[pl.ds(g * LANES + y, 8, stride=ROWS), :] for y in range(ROWS)]

    def halo_copies(turn):
        west_of, east_of = lax.rem(me + n_tile - 1, n_tile), lax.rem(me + 1, n_tile)
        plan = (
            (rows_out.at[turn, 0], rows_in.at[turn, 1], (north, me)),
            (rows_out.at[turn, 1], rows_in.at[turn, 0], (south, me)),
            (cols_out.at[turn, 0], cols_in.at[turn, 1], (comp, west_of)),
            (cols_out.at[turn, 1], cols_in.at[turn, 0], (comp, east_of)),
        )
        return [
            pltpu.make_async_remote_copy(
                src_ref=src,
                dst_ref=dst,
                send_sem=halo_send.at[turn, i],
                recv_sem=halo_recv.at[turn, i],
                device_id=to,
                device_id_type=MESH,
            )
            for i, (src, dst, to) in enumerate(plan)
        ]

    keep_north = (comp > 0).astype(F32)
    keep_south = (comp < n_comp - 1).astype(F32)

    def relax_group(g, source, target, turn):
        rows = group_rows(source, g)
        own8 = pl.ds(pl.multiple_of(g * 8, 8), 8)
        above = rows_in[turn, 0, own8, :] * keep_north
        below = rows_in[turn, 1, own8, :] * keep_south
        at = pl.ds(pl.multiple_of(g // 8 * 8, 8), 8)
        shift = lax.rem(LANES - lax.rem(g, 8) * ROWS, LANES)
        west = pltpu.roll(cols_in[turn, 0, at, :], shift, 1)
        east = pltpu.roll(cols_in[turn, 1, at, :], shift, 1)
        spread = rate[own8, :]
        new = []
        for y in range(ROWS):
            row = rows[y]
            left = pltpu.roll(
                jnp.where(lane8 == LANES - 1, pltpu.roll(west, LANES - 1 - y, 1), row), 1, 1
            )
            beyond = east if y == 0 else pltpu.roll(east, LANES - y, 1)
            right = pltpu.roll(jnp.where(lane8 == 0, beyond, row), LANES - 1, 1)
            up = above if y == 0 else rows[y - 1]
            down = below if y == ROWS - 1 else rows[y + 1]
            value = row + spread * (up + down + left + right - 4.0 * row)
            target[pl.ds(g * LANES + y, 8, stride=ROWS), :] = value
            new.append(value)
        return new

    cols_out[...] = jnp.zeros_like(cols_out)
    for copy in rest_loads:
        copy.wait()

    def first_pack(g, carry):
        pack(g, group_rows(state, g), 0)
        return carry

    lax.fori_loop(0, groups, first_pack, 0)
    halo_first = halo_copies(0)
    for copy in halo_first:
        copy.start()

    rate[pl.ds(0, ch_a), :] = jnp.broadcast_to(as_column(atm_rate[...], ch_a), (ch_a, LANES))
    rate[pl.ds(ch_a, ch_o), :] = jnp.broadcast_to(as_column(ocean_rate[...], ch_o), (ch_o, LANES))

    per = min(8, n_tile)
    parts = n_tile // per
    pltpu.make_async_copy(meta_in, meta_in, meta_recv).wait()
    for part in range(parts):
        total = meta_in[pl.ds(part * per * 8, 8), :]
        for d in range(1, per):
            total = total + meta_in[pl.ds((part * per + d) * 8, 8), :]
        asked_v[pl.ds(part * 8, 8), :] = total
    asked_copy = pltpu.make_async_copy(asked_v, asked_s, asked_sem)
    asked_copy.start()

    def build_onehot():
        shape = (2 * s_rows, LANES)
        y_at = rows_of(shape) & 15
        same = (rows_of(shape) >> 4) == (lanes_of(shape) & 15)
        for part in range(parts):
            total = asked_v[pl.ds(part * 8, 8), :]
            for r in range(CAP):
                hit = jnp.logical_and(same, jnp.broadcast_to(total[r : r + 1, :], shape) == y_at)
                start = r * n_tile * ROWS + part * LANES
                onehot[:, start : start + LANES] = jnp.where(hit, 1.0, 0.0).astype(BF16)

    top = rows_of((ROWS, LANES)) < 8

    def over_peers(fill, send):
        def far_to_near(i, carry):
            away = hops - (i + 1) // 2
            away = jnp.where(lax.rem(i, 2) == 1, away, n_z - away)
            other = lax.rem(z + away, n_z) * 2
            for k in range(2):
                fill(other + k)
                send(other + k)
            return carry

        lax.fori_loop(0, n_z - 1, far_to_near, 0)
        fill(sibling)
        send(sibling)
        fill(me)

    def pick(d):
        for r in range(CAP):
            row, lane = d // per * 8 + r, lax.rem(d, per) * ROWS
            sea = asked_s[row, lane] & 15
            air = asked_s[row, lane + 8] & 15
            tile_out[d * CAP + r] = jnp.where(top, own[air], own[sea])

    def send_tiles(d):
        pltpu.make_async_remote_copy(
            src_ref=tile_out.at[pl.ds(d * CAP, CAP)],
            dst_ref=tile_in.at[pl.ds(me * CAP, CAP)],
            send_sem=tile_send,
            recv_sem=tile_recv,
            device_id=(comp, d),
            device_id_type=MESH,
        ).start()

    def first_step(g, carry):
        pack(g, relax_group(g, state, middle, 0), 1)
        return carry

    def second_step(g, carry):
        relax_group(g, middle, result, 1)
        return carry

    asked_copy.wait()
    over_peers(pick, send_tiles)
    pltpu.make_async_copy(
        tile_out.at[pl.ds(me * CAP, CAP)], tile_in.at[pl.ds(me * CAP, CAP)], tile_recv
    ).start()

    build_onehot()
    for copy in halo_first:
        copy.wait()
    lax.fori_loop(0, groups, first_step, 0, unroll=2)
    halo_second = halo_copies(1)
    for copy in halo_second:
        copy.start()
    def write(i, src_row, dst, dst_row, size):
        copy = pltpu.make_async_copy(
            result.at[pl.ds(src_row, size)], dst.at[pl.ds(dst_row, size)], out_sem.at[i]
        )
        copy.start()
        return copy

    weight_load.wait()
    table_copy.wait()
    pltpu.make_async_copy(tile_in, tile_in, tile_recv).wait()

    def msg_slot(e):
        return pl.ds(pl.multiple_of(e * ROWS, ROWS), ROWS)

    def fill(e):
        for r in range(CAP):
            s = e * 8 + r
            ahead = jnp.dot(
                tile_in[table_s[1, s]], weight[table_s[0, s]], preferred_element_type=F32
            )
            back = lax.dot_general(
                tile_in[table_s[3, s]],
                weight[table_s[2, s]],
                (((1,), (1,)), ((), ())),
                preferred_element_type=F32,
            )
            msg_out[msg_slot(e), r * LANES : (r + 1) * LANES] = jnp.where(top, ahead, back).astype(
                BF16
            )

    def send(e):
        pltpu.make_async_remote_copy(
            src_ref=msg_out.at[msg_slot(e)],
            dst_ref=msg_in.at[msg_slot(me)],
            send_sem=msg_send,
            recv_sem=msg_recv,
            device_id=(comp, e),
            device_id_type=MESH,
        ).start()

    over_peers(fill, send)
    pltpu.make_async_copy(msg_out.at[msg_slot(me)], msg_in.at[msg_slot(me)], msg_recv).start()

    for copy in halo_second:
        copy.wait()
    lax.fori_loop(0, groups, second_step, 0, unroll=2)

    writes = [write(0, s_rows, atm_out, s_rows, a_rows - s_rows)]
    if ch_o > SURF:
        writes.append(write(1, a_rows + s_rows, ocean_out, s_rows, ch_o * ROWS - s_rows))

    pltpu.make_async_copy(msg_in, msg_in, msg_recv).wait()
    force = jnp.zeros((2 * s_rows, LANES), F32)
    depth = n_tile * ROWS
    for r in range(CAP):
        force = force + jnp.dot(
            onehot[:, r * depth : (r + 1) * depth],
            msg_in[:, r * LANES : (r + 1) * LANES],
            preferred_element_type=F32,
        )
    wet_rows = jnp.concatenate([wet] * SURF, axis=0)
    result[pl.ds(0, s_rows), :] = result[pl.ds(0, s_rows), :] + force[s_rows:]
    writes.append(write(2, 0, atm_out, 0, s_rows))
    result[pl.ds(a_rows, s_rows), :] = result[pl.ds(a_rows, s_rows), :] + force[:s_rows] * wet_rows
    writes.append(write(3, a_rows, ocean_out, 0, s_rows))

    tiles = tile_out.at[pl.ds(0, (n_tile - 1) * CAP)]
    pltpu.make_async_copy(tiles, tiles, tile_send).wait()
    metas = meta_out.at[pl.ds(0, (n_tile - 1) * 8)]
    pltpu.make_async_copy(metas, metas, meta_send).wait()
    msgs = msg_out.at[pl.ds(0, (n_tile - 1) * ROWS)]
    pltpu.make_async_copy(msgs, msgs, msg_send).wait()
    for copy in writes:
        copy.wait()


def hand_over(atm, ocean, atm_out, ocean_out, atm_held, ocean_held, in_sem, out_sem):
    arrivals, departures = [], []
    for source, held, target, parts in (
        (atm, atm_held, atm_out, 8),
        (ocean, ocean_held, ocean_out, 3),
    ):
        size = source.shape[0] // parts
        for part in range(parts):
            rows, i = pl.ds(part * size, size), len(arrivals)
            arrivals.append(pltpu.make_async_copy(source.at[rows], held.at[rows], in_sem.at[i]))
            departures.append(pltpu.make_async_copy(held.at[rows], target.at[rows], out_sem.at[i]))
    for copy in arrivals:
        copy.start()
    for arrival, departure in zip(arrivals, departures):
        arrival.wait()
        departure.start()
    for copy in departures:
        copy.wait()


def shards(
    n_comp,
    n_tile,
    atm_state,
    ocean_state,
    atm_rate,
    ocean_rate,
    ocean_mask,
    remap_weight,
    pair_src,
    pair_tgt,
    pair_count,
):
    ch_a, ch_o = atm_state.shape[0], ocean_state.shape[0]
    pairs = pair_src.shape[1]
    total = ch_a + ch_o
    a_rows, o_rows = ch_a * ROWS, ch_o * ROWS
    packed = (total // 8 + 7) // 8 * 8
    hbm = pl.BlockSpec(memory_space=pltpu.HBM)
    dma = pltpu.SemaphoreType.DMA
    atm_next, ocean_next = pl.pallas_call(
        functools.partial(kernel, (n_comp, n_tile, ch_a, ch_o, pairs)),
        out_shape=(
            jax.ShapeDtypeStruct((a_rows, LANES), F32),
            jax.ShapeDtypeStruct((o_rows, LANES), F32),
        ),
        in_specs=[hbm] * 8 + [pl.BlockSpec(memory_space=pltpu.SMEM)],
        out_specs=(hbm, hbm),
        scratch_shapes=[
            pltpu.VMEM((total * ROWS + ROWS, LANES), F32),
            pltpu.VMEM((total * ROWS + ROWS, LANES), F32),
            pltpu.VMEM((total * ROWS + ROWS, LANES), F32),
            pltpu.VMEM((pairs, LANES, LANES), BF16),
            pltpu.VMEM((1, ch_a), F32),
            pltpu.VMEM((1, ch_o), F32),
            pltpu.VMEM((1, ROWS), jnp.int32),
            pltpu.VMEM((1, pairs), jnp.int32),
            pltpu.VMEM((1, pairs), jnp.int32),
            pltpu.VMEM((ROWS, 2 * SURF, LANES), BF16),
            pltpu.VMEM((n_tile * CAP, 2 * SURF, LANES), BF16),
            pltpu.VMEM((n_tile * CAP, 2 * SURF, LANES), BF16),
            pltpu.VMEM((n_tile * ROWS, CAP * LANES), BF16),
            pltpu.VMEM((n_tile * ROWS, CAP * LANES), BF16),
            pltpu.VMEM((n_tile * 8, LANES), jnp.int32),
            pltpu.VMEM((n_tile * 8, LANES), jnp.int32),
            pltpu.VMEM((2 * SURF * ROWS, CAP * n_tile * ROWS), BF16),
            pltpu.VMEM((total, LANES), F32),
            pltpu.VMEM((2, 2, total, LANES), F32),
            pltpu.VMEM((2, 2, total, LANES), F32),
            pltpu.VMEM((2, 2, packed, LANES), F32),
            pltpu.VMEM((2, 2, packed, LANES), F32),
            pltpu.VMEM((8, n_tile * 8), jnp.int32),
            pltpu.SMEM((8, n_tile * 8), jnp.int32),
            pltpu.VMEM(((n_tile + 7) // 8 * 8, LANES), jnp.int32),
            pltpu.SMEM(((n_tile + 7) // 8 * 8, LANES), jnp.int32),
            dma((10,)),
            dma,
            dma,
            dma((2, 4)),
            dma((2, 4)),
            dma,
            dma,
            dma,
            dma,
            dma,
            dma,
            dma((4,)),
        ],
        compiler_params=pltpu.CompilerParams(
            collective_id=0, has_side_effects=True, vmem_limit_bytes=60 * 1024 * 1024
        ),
        name="coupled_interval",
    )(
        atm_state.reshape(a_rows, LANES),
        ocean_state.reshape(o_rows, LANES),
        atm_rate.reshape(1, ch_a),
        ocean_rate.reshape(1, ch_o),
        ocean_mask.reshape(1, ROWS),
        remap_weight.reshape(pairs, LANES, LANES),
        pair_src,
        pair_tgt,
        pair_count,
    )
    atm_next, ocean_next = pl.pallas_call(
        hand_over,
        out_shape=(
            jax.ShapeDtypeStruct((a_rows, LANES), F32),
            jax.ShapeDtypeStruct((o_rows, LANES), F32),
        ),
        in_specs=[hbm, hbm],
        out_specs=(hbm, hbm),
        scratch_shapes=[
            pltpu.VMEM((a_rows, LANES), F32),
            pltpu.VMEM((o_rows, LANES), F32),
            dma((11,)),
            dma((11,)),
        ],
        compiler_params=pltpu.CompilerParams(vmem_limit_bytes=60 * 1024 * 1024),
        name="hand_over",
    )(atm_next, ocean_next)
    return atm_next.reshape(ch_a, ROWS, LANES), ocean_next.reshape(ch_o, ROWS, LANES)


def solution(mesh):
    return jax.shard_map(
        functools.partial(shards, mesh.shape["comp"], mesh.shape["tile"]),
        mesh=mesh,
        in_specs=(
            P(None, "comp", "tile"),
            P(None, "comp", "tile"),
            P(),
            P(),
            P("comp", "tile"),
            P("comp", "tile", None, None),
            P("comp", "tile"),
            P("comp", "tile"),
            P("comp", "tile"),
        ),
        out_specs=(P(None, "comp", "tile"), P(None, "comp", "tile")),
        check_vma=False,
    )
```

```python
import functools

import jax
import jax.numpy as jnp
from jax import lax
from jax.experimental import pallas as pl
from jax.experimental.pallas import tpu as pltpu
from jax.sharding import PartitionSpec as P

SURF = 8
LANES = 128
ROWS = 16
CAP = 3
EMPTY = 16
F32 = jnp.float32
BF16 = jnp.bfloat16
MESH = pl.DeviceIdType.MESH


def lanes_of(shape):
    return lax.broadcasted_iota(jnp.int32, shape, 1)


def rows_of(shape):
    return lax.broadcasted_iota(jnp.int32, shape, 0)


def as_column(row, size):
    shape = (size, size)
    spread = jnp.broadcast_to(row, shape)
    zero = jnp.zeros(shape, row.dtype)
    return jnp.sum(jnp.where(rows_of(shape) == lanes_of(shape), spread, zero), axis=1, keepdims=True)


def as_row(column, size):
    shape = (size, size)
    spread = jnp.broadcast_to(column, shape)
    zero = jnp.zeros(shape, column.dtype)
    return jnp.sum(jnp.where(rows_of(shape) == lanes_of(shape), spread, zero), axis=0, keepdims=True)


def kernel(
    sizes,
    atm_hbm,
    ocean_hbm,
    atm_rate_hbm,
    ocean_rate_hbm,
    mask_hbm,
    weight_hbm,
    pair_src_hbm,
    pair_tgt_hbm,
    pair_count,
    atm_out,
    ocean_out,
    state,
    middle,
    result,
    weight,
    atm_rate,
    ocean_rate,
    mask,
    pair_src,
    pair_tgt,
    own,
    tile_out,
    tile_in,
    msg_out,
    msg_in,
    meta_out,
    meta_in,
    onehot,
    rate,
    rows_out,
    rows_in,
    cols_out,
    cols_in,
    table_v,
    table_s,
    asked_v,
    asked_s,
    load_sem,
    tile_send,
    tile_recv,
    halo_send,
    halo_recv,
    meta_send,
    meta_recv,
    msg_send,
    msg_recv,
    table_sem,
    asked_sem,
    out_sem,
):
    n_comp, n_tile, ch_a, ch_o, pairs = sizes
    n_z = n_tile // 2
    hops = n_z // 2
    groups = (ch_a + ch_o) // 8
    a_rows = ch_a * ROWS
    all_rows = (ch_a + ch_o) * ROWS
    s_rows = SURF * ROWS
    slots = n_tile * 8
    comp = lax.axis_index("comp")
    me = lax.axis_index("tile")
    z = me // 2
    core = me % 2
    sibling = z * 2 + 1 - core

    def load(i, src, dst):
        copy = pltpu.make_async_copy(src, dst, load_sem.at[i])
        copy.start()
        return copy

    surf_loads = (
        load(5, mask_hbm, mask),
        load(0, atm_hbm.at[pl.ds(0, s_rows)], state.at[pl.ds(0, s_rows)]),
        load(1, ocean_hbm.at[pl.ds(0, s_rows)], state.at[pl.ds(a_rows, s_rows)]),
    )
    rest_loads = [
        load(2, atm_hbm.at[pl.ds(s_rows, a_rows - s_rows)], state.at[pl.ds(s_rows, a_rows - s_rows)])
    ]
    if ch_o > SURF:
        rest_loads.append(
            load(
                3,
                ocean_hbm.at[pl.ds(s_rows, ch_o * ROWS - s_rows)],
                state.at[pl.ds(a_rows + s_rows, ch_o * ROWS - s_rows)],
            )
        )
    small_loads = [
        load(6, atm_rate_hbm, atm_rate),
        load(7, ocean_rate_hbm, ocean_rate),
        load(8, pair_src_hbm, pair_src),
        load(9, pair_tgt_hbm, pair_tgt),
    ]
    weight_load = load(4, weight_hbm, weight)

    barrier = pltpu.get_barrier_semaphore()
    north = lax.rem(comp + n_comp - 1, n_comp)
    south = lax.rem(comp + 1, n_comp)

    def greet(i, carry):
        pl.semaphore_signal(
            barrier, inc=1, device_id=(comp, lax.rem(me + i, n_tile)), device_id_type=MESH
        )
        return carry

    lax.fori_loop(1, n_tile, greet, 0)
    pl.semaphore_signal(barrier, inc=1, device_id=(north, me), device_id_type=MESH)
    pl.semaphore_signal(barrier, inc=1, device_id=(south, me), device_id_type=MESH)

    for copy in small_loads:
        copy.wait()

    pair_shape = (pairs, pairs)
    later = lanes_of(pair_shape) < rows_of(pair_shape)
    live_row = (lanes_of((1, pairs)) < pair_count[0, 0]).astype(jnp.int32)
    live_column = (rows_of((pairs, 1)) < pair_count[0, 0]).astype(jnp.int32)
    live_all = jnp.broadcast_to(live_row, pair_shape)
    pair_column = rows_of((pairs, 1))
    slot_lane = lanes_of((pairs, slots))
    slot_row = rows_of((slots, pairs))
    place, lines, y_of = [], [], []
    for codes in (pair_tgt, pair_src):
        code = codes[...]
        peer = code >> 4
        y_row = code & 15
        peer_column = as_column(peer, pairs)
        before = jnp.logical_and(later, jnp.broadcast_to(peer, pair_shape) == peer_column)
        rank_column = jnp.sum(
            jnp.where(before, live_all, jnp.zeros_like(live_all)), axis=1, keepdims=True
        )
        rank_row = as_row(rank_column, pairs)
        slot_column = jnp.where(live_column > 0, peer_column * 8 + rank_column, -1)
        slot_of_row = jnp.where(live_row > 0, peer * 8 + rank_row, -1)
        place.append(peer_column * CAP + rank_column)
        lines.append(slot_column == slot_lane)
        hot_rows = jnp.where(slot_row == slot_of_row, jnp.broadcast_to(y_row - EMPTY, (slots, pairs)), jnp.zeros_like(slot_row))
        y_of.append(jnp.sum(hot_rows, axis=1, keepdims=True) + EMPTY)
    meta_lane = lanes_of((slots, LANES))
    inside = (meta_lane >> 4) == lax.rem(me, 8)
    meta_out[...] = jnp.where(
        inside,
        jnp.where(
            (meta_lane & 15) < 8,
            jnp.broadcast_to(y_of[0], (slots, LANES)),
            jnp.broadcast_to(y_of[1], (slots, LANES)),
        ),
        jnp.zeros_like(meta_lane),
    )

    def meta_slot(e):
        return pl.ds(pl.multiple_of(e * 8, 8), 8)

    def send_meta(i, carry):
        e = lax.rem(me + i, n_tile)
        pltpu.make_async_remote_copy(
            src_ref=meta_out.at[meta_slot(e)],
            dst_ref=meta_in.at[meta_slot(me)],
            send_sem=meta_send,
            recv_sem=meta_recv,
            device_id=(comp, e),
            device_id_type=MESH,
        ).start()
        return carry

    pl.semaphore_wait(barrier, n_tile + 1)
    lax.fori_loop(1, n_tile, send_meta, 0)
    pltpu.make_async_copy(
        meta_out.at[meta_slot(me)], meta_in.at[meta_slot(me)], meta_recv
    ).start()

    for copy in surf_loads:
        copy.wait()
    wet = jnp.broadcast_to(as_column(mask[...].astype(F32), ROWS), (ROWS, LANES))
    for y in range(ROWS):
        air = state[pl.ds(y, 8, stride=ROWS), :]
        sea = state[pl.ds(a_rows + y, 8, stride=ROWS), :] * wet[y : y + 1, :]
        own[y] = jnp.concatenate([air, sea], axis=0).astype(BF16)


    lane8 = lanes_of((8, LANES))

    def pack(g, rows, turn):
        west = jnp.zeros((8, LANES), F32)
        east = jnp.zeros((8, LANES), F32)
        for y in range(ROWS):
            here = lane8 == y
            west = jnp.where(here, rows[y] if y == 0 else pltpu.roll(rows[y], y, 1), west)
            east = jnp.where(here, pltpu.roll(rows[y], y + 1, 1), east)
        shift = lax.rem(g, 8) * ROWS
        at = pl.ds(pl.multiple_of(g // 8 * 8, 8), 8)
        cols_out[turn, 0, at, :] = cols_out[turn, 0, at, :] + pltpu.roll(west, shift, 1)
        cols_out[turn, 1, at, :] = cols_out[turn, 1, at, :] + pltpu.roll(east, shift, 1)
        own8 = pl.ds(pl.multiple_of(g * 8, 8), 8)
        rows_out[turn, 0, own8, :] = rows[0]
        rows_out[turn, 1, own8, :] = rows[ROWS - 1]

    def group_rows(ref, g):
        return [ref[pl.ds(g * LANES + y, 8, stride=ROWS), :] for y in range(ROWS)]

    def halo_copies(turn):
        west_of, east_of = lax.rem(me + n_tile - 1, n_tile), lax.rem(me + 1, n_tile)
        plan = (
            (rows_out.at[turn, 0], rows_in.at[turn, 1], (north, me)),
            (rows_out.at[turn, 1], rows_in.at[turn, 0], (south, me)),
            (cols_out.at[turn, 0], cols_in.at[turn, 1], (comp, west_of)),
            (cols_out.at[turn, 1], cols_in.at[turn, 0], (comp, east_of)),
        )
        return [
            pltpu.make_async_remote_copy(
                src_ref=src,
                dst_ref=dst,
                send_sem=halo_send.at[turn, i],
                recv_sem=halo_recv.at[turn, i],
                device_id=to,
                device_id_type=MESH,
            )
            for i, (src, dst, to) in enumerate(plan)
        ]

    keep_north = (comp > 0).astype(F32)
    keep_south = (comp < n_comp - 1).astype(F32)

    def relax_group(g, source, target, turn):
        rows = group_rows(source, g)
        own8 = pl.ds(pl.multiple_of(g * 8, 8), 8)
        above = rows_in[turn, 0, own8, :] * keep_north
        below = rows_in[turn, 1, own8, :] * keep_south
        at = pl.ds(pl.multiple_of(g // 8 * 8, 8), 8)
        shift = lax.rem(LANES - lax.rem(g, 8) * ROWS, LANES)
        west = pltpu.roll(cols_in[turn, 0, at, :], shift, 1)
        east = pltpu.roll(cols_in[turn, 1, at, :], shift, 1)
        spread = rate[own8, :]
        new = []
        for y in range(ROWS):
            row = rows[y]
            left = pltpu.roll(
                jnp.where(lane8 == LANES - 1, pltpu.roll(west, LANES - 1 - y, 1), row), 1, 1
            )
            beyond = east if y == 0 else pltpu.roll(east, LANES - y, 1)
            right = pltpu.roll(jnp.where(lane8 == 0, beyond, row), LANES - 1, 1)
            up = above if y == 0 else rows[y - 1]
            down = below if y == ROWS - 1 else rows[y + 1]
            value = row + spread * (up + down + left + right - 4.0 * row)
            target[pl.ds(g * LANES + y, 8, stride=ROWS), :] = value
            new.append(value)
        return new

    cols_out[...] = jnp.zeros_like(cols_out)
    for copy in rest_loads:
        copy.wait()

    def first_pack(g, carry):
        pack(g, group_rows(state, g), 0)
        return carry

    lax.fori_loop(0, groups, first_pack, 0)
    halo_first = halo_copies(0)
    for copy in halo_first:
        copy.start()

    per = min(8, n_tile)
    parts = n_tile // per
    pltpu.make_async_copy(meta_in, meta_in, meta_recv).wait()
    for part in range(parts):
        total = meta_in[pl.ds(part * per * 8, 8), :]
        for d in range(1, per):
            total = total + meta_in[pl.ds((part * per + d) * 8, 8), :]
        asked_v[pl.ds(part * 8, 8), :] = total
    asked_copy = pltpu.make_async_copy(asked_v, asked_s, asked_sem)
    asked_copy.start()

    def build_onehot():
        shape = (2 * s_rows, LANES)
        y_at = rows_of(shape) & 15
        same = (rows_of(shape) >> 4) == (lanes_of(shape) & 15)
        for part in range(parts):
            total = asked_v[pl.ds(part * 8, 8), :]
            for r in range(CAP):
                hit = jnp.logical_and(same, jnp.broadcast_to(total[r : r + 1, :], shape) == y_at)
                start = r * n_tile * ROWS + part * LANES
                onehot[:, start : start + LANES] = jnp.where(hit, 1.0, 0.0).astype(BF16)

    top = rows_of((ROWS, LANES)) < 8

    def over_peers(fill, send):
        def far_to_near(i, carry):
            away = hops - (i + 1) // 2
            away = jnp.where(lax.rem(i, 2) == 1, away, n_z - away)
            other = lax.rem(z + away, n_z) * 2
            for k in range(2):
                fill(other + k)
                send(other + k)
            return carry

        lax.fori_loop(0, n_z - 1, far_to_near, 0)
        fill(sibling)
        send(sibling)
        fill(me)

    def pick(d):
        for r in range(CAP):
            row, lane = d // per * 8 + r, lax.rem(d, per) * ROWS
            sea = asked_s[row, lane] & 15
            air = asked_s[row, lane + 8] & 15
            tile_out[d * CAP + r] = jnp.where(top, own[air], own[sea])

    def send_tiles(d):
        pltpu.make_async_remote_copy(
            src_ref=tile_out.at[pl.ds(d * CAP, CAP)],
            dst_ref=tile_in.at[pl.ds(me * CAP, CAP)],
            send_sem=tile_send,
            recv_sem=tile_recv,
            device_id=(comp, d),
            device_id_type=MESH,
        ).start()

    def first_step(g, carry):
        pack(g, relax_group(g, state, middle, 0), 1)
        return carry

    def second_step(g, carry):
        relax_group(g, middle, result, 1)
        return carry

    asked_copy.wait()
    over_peers(pick, send_tiles)
    pltpu.make_async_copy(
        tile_out.at[pl.ds(me * CAP, CAP)], tile_in.at[pl.ds(me * CAP, CAP)], tile_recv
    ).start()

    table_v[...] = jnp.zeros_like(table_v)
    for i, (hot, values) in enumerate(
        ((lines[0], pair_column), (lines[0], place[1]), (lines[1], pair_column), (lines[1], place[0]))
    ):
        found = jnp.where(hot, jnp.broadcast_to(values, (pairs, slots)), jnp.zeros_like(slot_lane))
        table_v[i : i + 1, :] = jnp.sum(found, axis=0, keepdims=True)
    table_copy = pltpu.make_async_copy(table_v, table_s, table_sem)
    table_copy.start()
    rate[pl.ds(0, ch_a), :] = jnp.broadcast_to(as_column(atm_rate[...], ch_a), (ch_a, LANES))
    rate[pl.ds(ch_a, ch_o), :] = jnp.broadcast_to(as_column(ocean_rate[...], ch_o), (ch_o, LANES))

    build_onehot()
    for copy in halo_first:
        copy.wait()
    lax.fori_loop(0, groups, first_step, 0, unroll=2)
    halo_second = halo_copies(1)
    for copy in halo_second:
        copy.start()
    def write(i, src_row, dst, dst_row, size):
        copy = pltpu.make_async_copy(
            result.at[pl.ds(src_row, size)], dst.at[pl.ds(dst_row, size)], out_sem.at[i]
        )
        copy.start()
        return copy

    weight_load.wait()
    table_copy.wait()
    pltpu.make_async_copy(tile_in, tile_in, tile_recv).wait()

    def msg_slot(e):
        return pl.ds(pl.multiple_of(e * ROWS, ROWS), ROWS)

    def fill(e):
        for r in range(CAP):
            s = e * 8 + r
            ahead = jnp.dot(
                tile_in[table_s[1, s]], weight[table_s[0, s]], preferred_element_type=F32
            )
            back = lax.dot_general(
                tile_in[table_s[3, s]],
                weight[table_s[2, s]],
                (((1,), (1,)), ((), ())),
                preferred_element_type=F32,
            )
            msg_out[msg_slot(e), r * LANES : (r + 1) * LANES] = jnp.where(top, ahead, back).astype(
                BF16
            )

    def send(e):
        pltpu.make_async_remote_copy(
            src_ref=msg_out.at[msg_slot(e)],
            dst_ref=msg_in.at[msg_slot(me)],
            send_sem=msg_send,
            recv_sem=msg_recv,
            device_id=(comp, e),
            device_id_type=MESH,
        ).start()

    over_peers(fill, send)
    pltpu.make_async_copy(msg_out.at[msg_slot(me)], msg_in.at[msg_slot(me)], msg_recv).start()

    for copy in halo_second:
        copy.wait()
    lax.fori_loop(0, groups, second_step, 0, unroll=2)

    writes = [write(0, s_rows, atm_out, s_rows, a_rows - s_rows)]
    if ch_o > SURF:
        writes.append(write(1, a_rows + s_rows, ocean_out, s_rows, ch_o * ROWS - s_rows))

    pltpu.make_async_copy(msg_in, msg_in, msg_recv).wait()
    force = jnp.zeros((2 * s_rows, LANES), F32)
    depth = n_tile * ROWS
    for r in range(CAP):
        force = force + jnp.dot(
            onehot[:, r * depth : (r + 1) * depth],
            msg_in[:, r * LANES : (r + 1) * LANES],
            preferred_element_type=F32,
        )
    wet_rows = jnp.concatenate([wet] * SURF, axis=0)
    result[pl.ds(0, s_rows), :] = result[pl.ds(0, s_rows), :] + force[s_rows:]
    writes.append(write(2, 0, atm_out, 0, s_rows))
    result[pl.ds(a_rows, s_rows), :] = result[pl.ds(a_rows, s_rows), :] + force[:s_rows] * wet_rows
    writes.append(write(3, a_rows, ocean_out, 0, s_rows))

    tiles = tile_out.at[pl.ds(0, (n_tile - 1) * CAP)]
    pltpu.make_async_copy(tiles, tiles, tile_send).wait()
    metas = meta_out.at[pl.ds(0, (n_tile - 1) * 8)]
    pltpu.make_async_copy(metas, metas, meta_send).wait()
    msgs = msg_out.at[pl.ds(0, (n_tile - 1) * ROWS)]
    pltpu.make_async_copy(msgs, msgs, msg_send).wait()
    for copy in writes:
        copy.wait()


def hand_over(atm, ocean, atm_out, ocean_out, atm_held, ocean_held, in_sem, out_sem):
    arrivals, departures = [], []
    for source, held, target, parts in (
        (atm, atm_held, atm_out, 8),
        (ocean, ocean_held, ocean_out, 3),
    ):
        size = source.shape[0] // parts
        for part in range(parts):
            rows, i = pl.ds(part * size, size), len(arrivals)
            arrivals.append(pltpu.make_async_copy(source.at[rows], held.at[rows], in_sem.at[i]))
            departures.append(pltpu.make_async_copy(held.at[rows], target.at[rows], out_sem.at[i]))
    for copy in arrivals:
        copy.start()
    for arrival, departure in zip(arrivals, departures):
        arrival.wait()
        departure.start()
    for copy in departures:
        copy.wait()


def shards(
    n_comp,
    n_tile,
    atm_state,
    ocean_state,
    atm_rate,
    ocean_rate,
    ocean_mask,
    remap_weight,
    pair_src,
    pair_tgt,
    pair_count,
):
    ch_a, ch_o = atm_state.shape[0], ocean_state.shape[0]
    pairs = pair_src.shape[1]
    total = ch_a + ch_o
    a_rows, o_rows = ch_a * ROWS, ch_o * ROWS
    packed = (total // 8 + 7) // 8 * 8
    hbm = pl.BlockSpec(memory_space=pltpu.HBM)
    dma = pltpu.SemaphoreType.DMA
    atm_next, ocean_next = pl.pallas_call(
        functools.partial(kernel, (n_comp, n_tile, ch_a, ch_o, pairs)),
        out_shape=(
            jax.ShapeDtypeStruct((a_rows, LANES), F32),
            jax.ShapeDtypeStruct((o_rows, LANES), F32),
        ),
        in_specs=[hbm] * 8 + [pl.BlockSpec(memory_space=pltpu.SMEM)],
        out_specs=(hbm, hbm),
        scratch_shapes=[
            pltpu.VMEM((total * ROWS + ROWS, LANES), F32),
            pltpu.VMEM((total * ROWS + ROWS, LANES), F32),
            pltpu.VMEM((total * ROWS + ROWS, LANES), F32),
            pltpu.VMEM((pairs, LANES, LANES), BF16),
            pltpu.VMEM((1, ch_a), F32),
            pltpu.VMEM((1, ch_o), F32),
            pltpu.VMEM((1, ROWS), jnp.int32),
            pltpu.VMEM((1, pairs), jnp.int32),
            pltpu.VMEM((1, pairs), jnp.int32),
            pltpu.VMEM((ROWS, 2 * SURF, LANES), BF16),
            pltpu.VMEM((n_tile * CAP, 2 * SURF, LANES), BF16),
            pltpu.VMEM((n_tile * CAP, 2 * SURF, LANES), BF16),
            pltpu.VMEM((n_tile * ROWS, CAP * LANES), BF16),
            pltpu.VMEM((n_tile * ROWS, CAP * LANES), BF16),
            pltpu.VMEM((n_tile * 8, LANES), jnp.int32),
            pltpu.VMEM((n_tile * 8, LANES), jnp.int32),
            pltpu.VMEM((2 * SURF * ROWS, CAP * n_tile * ROWS), BF16),
            pltpu.VMEM((total, LANES), F32),
            pltpu.VMEM((2, 2, total, LANES), F32),
            pltpu.VMEM((2, 2, total, LANES), F32),
            pltpu.VMEM((2, 2, packed, LANES), F32),
            pltpu.VMEM((2, 2, packed, LANES), F32),
            pltpu.VMEM((8, n_tile * 8), jnp.int32),
            pltpu.SMEM((8, n_tile * 8), jnp.int32),
            pltpu.VMEM(((n_tile + 7) // 8 * 8, LANES), jnp.int32),
            pltpu.SMEM(((n_tile + 7) // 8 * 8, LANES), jnp.int32),
            dma((10,)),
            dma,
            dma,
            dma((2, 4)),
            dma((2, 4)),
            dma,
            dma,
            dma,
            dma,
            dma,
            dma,
            dma((4,)),
        ],
        compiler_params=pltpu.CompilerParams(
            collective_id=0, has_side_effects=True, vmem_limit_bytes=60 * 1024 * 1024
        ),
        name="coupled_interval",
    )(
        atm_state.reshape(a_rows, LANES),
        ocean_state.reshape(o_rows, LANES),
        atm_rate.reshape(1, ch_a),
        ocean_rate.reshape(1, ch_o),
        ocean_mask.reshape(1, ROWS),
        remap_weight.reshape(pairs, LANES, LANES),
        pair_src,
        pair_tgt,
        pair_count,
    )
    atm_next, ocean_next = pl.pallas_call(
        hand_over,
        out_shape=(
            jax.ShapeDtypeStruct((a_rows, LANES), F32),
            jax.ShapeDtypeStruct((o_rows, LANES), F32),
        ),
        in_specs=[hbm, hbm],
        out_specs=(hbm, hbm),
        scratch_shapes=[
            pltpu.VMEM((a_rows, LANES), F32),
            pltpu.VMEM((o_rows, LANES), F32),
            dma((11,)),
            dma((11,)),
        ],
        compiler_params=pltpu.CompilerParams(vmem_limit_bytes=60 * 1024 * 1024),
        name="hand_over",
    )(atm_next, ocean_next)
    return atm_next.reshape(ch_a, ROWS, LANES), ocean_next.reshape(ch_o, ROWS, LANES)


def solution(mesh):
    return jax.shard_map(
        functools.partial(shards, mesh.shape["comp"], mesh.shape["tile"]),
        mesh=mesh,
        in_specs=(
            P(None, "comp", "tile"),
            P(None, "comp", "tile"),
            P(),
            P(),
            P("comp", "tile"),
            P("comp", "tile", None, None),
            P("comp", "tile"),
            P("comp", "tile"),
            P("comp", "tile"),
        ),
        out_specs=(P(None, "comp", "tile"), P(None, "comp", "tile")),
        check_vma=False,
    )
```
